32 devices in a mesh: energy: 4 (over z), cuts: 8 (over y, x, core).
Axes of the slice: x: 2, y: 2, z: 4, core: 2. Of those that a mesh axis runs over, the one named last changes fastest.
Arguments:
- coupling: bfloat16 [8, 720, 720], P('cuts'), may hold values from -0.3125 to 0.3125
- block_mask: int32 [8, 6, 6], P('cuts'), may hold values from 0 to 1, as said below
- levels: float32 [8, 720], P('cuts'), may hold values from -4 to 4
- dwell: float32 [8, 720], P('cuts'), may hold values from 0.5 to 3
- polarization: bfloat16 [2, 8, 8, 720, 720], P(None, 'energy', 'cuts'), may hold values from -6 to 6
Outputs:
- sigma: bfloat16 [2, 8, 8, 720, 720], P(None, 'energy', 'cuts')
The draws below stay inside these ranges and needn't reach their ends.
Inputs may be any that keep to these rules, and one draw needn't show every extreme that they name: `block_mask`: 1 where a coupling block of a slice is present, else 0; the diagonal blocks are always present.
All inputs are finite; a program needn't handle non-finite values.
Results may differ from the reference program's by a relative error of at most 0.023.
Values may be sent and summed in bfloat16 or wider, within the bound.
No kernel may reach another device: no remote copies, remote signals or barrier semaphores. Data moves between devices by JAX's collectives and lax.ppermute only.
A program may use at most 192 MiB of HBM per device.

```python
import math
import jax
import jax.numpy as jnp
from jax import lax

NO = 720
BLOCKS = 6
NE = 8
SLICES = 8


def draw_block_mask(key, part):
    random_bits = jax.random.randint(key, (SLICES, BLOCKS, BLOCKS), 0, 2)
    diagonal = jnp.eye(BLOCKS, dtype=jnp.int32)
    return jnp.maximum(random_bits, diagonal[None]).astype(jnp.int32)


def block_levels(key, extent, pieces, smallest, top_value):
    def one(position, shards_of):
        draws = jax.random.uniform(jax.random.fold_in(jax.random.fold_in(key, 6), position), (shards_of,), jnp.float32, smallest / len(pieces), top_value / len(pieces))
        return jnp.repeat(jnp.exp(draws), extent[position] // shards_of).reshape((-1,) + (1,) * (len(extent) - position - 1))

    level = one(*pieces[0])
    for cut in pieces[1:]:
        level = level * one(*cut)
    return level


def centred(own_key, extent, width, bound, pieces=(), kind=jnp.bfloat16):
    array = width * jax.random.normal(own_key, extent, jnp.float32)
    if pieces:
        array = array * block_levels(own_key, extent, pieces, -0.22, 0.18)
    return jnp.clip(array, -bound, bound).astype(kind)


def setup_inputs(seed: int = 0) -> dict:
    splits = jax.random.split(jax.random.key(seed), 6)
    coupling = centred(splits[0], (SLICES, NO, NO), (NO * 7 // 12) ** -0.5, 0.3125, ((0, 8),))
    block_mask = draw_block_mask(jax.random.fold_in(splits[5], 71), 0)
    levels = jnp.clip(jax.random.uniform(splits[2], (SLICES, NO), jnp.float32, -4.0, 4.0) * block_levels(splits[2], (SLICES, NO), ((0, 8),), -0.4, 0.0), -4.0, 4.0)
    dwell = jnp.clip(jnp.exp(math.log(3.0) - 1.7917595 * jax.random.uniform(splits[3], (SLICES, NO), jnp.float32) ** block_levels(splits[3], (SLICES, NO), ((0, 8),), -0.2, 0.2)), 0.5, 3.0)
    polarization = centred(splits[4], (2, NE, SLICES, NO, NO), 1.0, 6.0, ((1, 4), (2, 8)))
    return {"coupling": coupling, "block_mask": block_mask, "levels": levels, "dwell": dwell, "polarization": polarization}


def complex_step(left_real, left_imag, right_real, right_imag):
    left_real = left_real.astype(jnp.float32)
    left_imag = left_imag.astype(jnp.float32)
    right_real = right_real.astype(jnp.float32)
    right_imag = right_imag.astype(jnp.float32)
    real_part = jnp.einsum('eab,ebc->eac', left_real, right_real) - jnp.einsum('eab,ebc->eac', left_imag, right_imag)
    imag_part = jnp.einsum('eab,ebc->eac', left_real, right_imag) + jnp.einsum('eab,ebc->eac', left_imag, right_real)
    return (real_part.astype(jnp.bfloat16), imag_part.astype(jnp.bfloat16))

def convolve_direct(green_real, green_imag, polar_block):
    energy_count = green_real.shape[0]
    green_real = green_real.astype(jnp.float32)
    green_imag = green_imag.astype(jnp.float32)
    polar_real = polar_block[0].astype(jnp.float32)
    polar_imag = polar_block[1].astype(jnp.float32)
    total_real = jnp.zeros(green_real.shape, jnp.float32)
    total_imag = jnp.zeros(green_real.shape, jnp.float32)
    for offset in range(energy_count):
        shift_real = jnp.pad(green_real[:energy_count - offset], ((offset, 0), (0, 0), (0, 0)))
        shift_imag = jnp.pad(green_imag[:energy_count - offset], ((offset, 0), (0, 0), (0, 0)))
        total_real = total_real + shift_real * polar_real[offset] - shift_imag * polar_imag[offset]
        total_imag = total_imag + shift_real * polar_imag[offset] + shift_imag * polar_real[offset]
    factor = math.sqrt(NO / NE)
    return (jnp.stack([total_real, total_imag]) * factor).astype(jnp.bfloat16)

def reference(coupling, block_mask, levels, dwell, polarization):
    block_width = NO // block_mask.shape[1]
    energy = jnp.arange(NE).astype(jnp.float32)

    def slice_step(propagator, inputs):
        couple, mask_small, level_row, dwell_row, polar_block = inputs
        spread_mask = jnp.repeat(jnp.repeat(mask_small, block_width, axis=0), block_width, axis=1)
        masked = couple.astype(jnp.float32) * spread_mask.astype(jnp.float32)
        phases = (energy[:, None] - level_row[None, :]) * dwell_row[None, :]
        step_re = (jnp.cos(phases)[:, :, None] * masked[None]).astype(jnp.bfloat16)
        step_im = (-jnp.sin(phases)[:, :, None] * masked[None]).astype(jnp.bfloat16)
        green_real, green_imag = complex_step(step_re, step_im, propagator[0], propagator[1])
        sigma_block = convolve_direct(green_real, green_imag, polar_block)
        return ((green_real, green_imag), sigma_block)
    identity_tile = jnp.broadcast_to(jnp.eye(NO, dtype=jnp.bfloat16), (NE, NO, NO))
    start = (identity_tile, jnp.zeros((NE, NO, NO), jnp.bfloat16))
    polar_slices = jnp.moveaxis(polarization, 2, 0)
    final, sigma_slices = lax.scan(slice_step, start, (coupling, block_mask, levels, dwell, polar_slices))
    return jnp.moveaxis(sigma_slices, 0, 2)
```

```python
import functools
import math

import jax
import jax.numpy as jnp
from jax import lax
from jax.experimental import pallas as pl
from jax.experimental.pallas import tpu as pltpu
from jax.sharding import PartitionSpec as P

LANES = 128
VMEM_BYTES = 48 * 1024 * 1024


def row_step(rows):
    return 16 if rows % 16 == 0 else rows


def row_block(rows):
    for parts in (3, 5, 2):
        if rows % (16 * parts) == 0:
            return rows // parts
    return rows


def chain_kernel(energies, place, first, couple, turns, own, other, state):
    step = pl.program_id(0)
    last = jnp.maximum(place[1], place[2])

    def turned(real, imag, e):
        cosine = turns[0, :, 2 * e : 2 * e + 1]
        sine = turns[0, :, 2 * e + 1 : 2 * e + 2]
        if imag is None:
            return cosine * real, -sine * real
        return cosine * real + sine * imag, cosine * imag - sine * real

    def keep(e, pair):
        state[e, :, :LANES] = pair[0].astype(jnp.bfloat16)
        state[e, :, LANES:] = pair[1].astype(jnp.bfloat16)

    @pl.when(step == 0)
    def _():
        start = first[0].astype(jnp.float32)
        for e in range(energies):
            keep(e, turned(start, None, e))

    @pl.when(jnp.logical_and(step > 0, step <= last))
    def _():
        for e in range(energies):
            product = jnp.dot(couple[0], state[e], preferred_element_type=jnp.float32)
            keep(e, turned(product[:, :LANES], product[:, LANES:], e))

    @pl.when(step == place[1])
    def _():
        own[...] = state[...]

    @pl.when(step == place[2])
    def _():
        other[...] = state[...]


def chain(couplings, turns, place, energies):
    count, rows, _ = couplings.shape
    shape = (energies, rows, 2 * LANES)
    whole = pl.BlockSpec(shape, lambda i, s: (0, 0, 0))
    return pl.pallas_call(
        functools.partial(chain_kernel, energies),
        grid_spec=pltpu.PrefetchScalarGridSpec(
            num_scalar_prefetch=1,
            grid=(count,),
            in_specs=[
                pl.BlockSpec((1, rows, LANES), lambda i, s: (0, 0, s[0])),
                pl.BlockSpec((1, rows, rows), lambda i, s: (jnp.minimum(i, jnp.maximum(s[1], s[2])), 0, 0)),
                pl.BlockSpec((1, rows, 2 * energies), lambda i, s: (i, 0, 0)),
            ],
            out_specs=[whole, whole],
            scratch_shapes=[pltpu.VMEM(shape, jnp.bfloat16)],
        ),
        out_shape=[jax.ShapeDtypeStruct(shape, jnp.bfloat16)] * 2,
        compiler_params=pltpu.CompilerParams(vmem_limit_bytes=VMEM_BYTES),
        cost_estimate=pl.CostEstimate(flops=1024, bytes_accessed=1024, transcendentals=0),
        name="chain",
    )(place, couplings, couplings, turns)


def convolved(green, sources, slots, energies, start=None):
    out = []
    for e in range(slots):
        real, imag = (None, None) if start is None else start(e)
        for shift, values in sources:
            for w in range(slots):
                g = shift * slots + e - w
                if g < 0 or g >= energies:
                    continue
                gr, gi = green(g)
                pr, pi = values(w)
                a, b = gr * pr - gi * pi, gr * pi + gi * pr
                real, imag = (a, b) if real is None else (real + a, imag + b)
        out.append((real, imag))
    return out


def by_rows(rows, body):
    step = row_step(rows)

    def one(r, carry):
        body(pl.ds(pl.multiple_of(r * step, step), step))
        return carry

    lax.fori_loop(0, rows // step, one, 0, unroll=math.gcd(rows // step, 3))


def remembered(read):
    seen = {}

    def get(i):
        if i not in seen:
            seen[i] = tuple(part.astype(jnp.float32) for part in read(i))
        return seen[i]

    return get


def conv_kernel(plan, place, mine, theirs, own, *refs):
    slots, energies, factor, sources, arrived, later, first_source = plan
    received, sums, out = refs[:sources], refs[sources : sources + arrived], refs[-1]

    def body(green_ref):
        def block(rows):
            green = remembered(lambda g: (green_ref[g, rows, :LANES], green_ref[g, rows, LANES:]))
            terms = [(0, remembered(lambda w: (own[0, w, 0, rows, :], own[1, w, 0, rows, :])))]
            for shift, ref in enumerate(received, 1):
                terms.append((shift, remembered(lambda w, ref=ref: (ref[0, 0, w, rows, :], ref[0, 1, w, rows, :]))))
            if not later:
                for e, (real, imag) in enumerate(convolved(green, terms, slots, energies)):
                    real, imag = real * factor, imag * factor
                    for got in sums:
                        real = real + got[0, 0, 0, e, rows, :].astype(jnp.float32)
                        imag = imag + got[0, 0, 1, e, rows, :].astype(jnp.float32)
                    out[0, e, 0, rows, :] = real.astype(out.dtype)
                    out[1, e, 0, rows, :] = imag.astype(out.dtype)
            for hop in range(later):
                ahead = [(hop + 1 + shift, values) for shift, values in terms]
                for e, (real, imag) in enumerate(convolved(green, ahead, slots, energies)):
                    real, imag = real * factor, imag * factor
                    for got in sums:
                        real = real + got[0, hop + 1, 0, e, rows, :].astype(jnp.float32)
                        imag = imag + got[0, hop + 1, 1, e, rows, :].astype(jnp.float32)
                    out[0, hop, 0, e, rows, :] = real.astype(out.dtype)
                    out[0, hop, 1, e, rows, :] = imag.astype(out.dtype)

        by_rows(own.shape[3], block)

    here = pl.program_id(0) == place[3]
    pl.when(here)(lambda: body(mine))
    pl.when(jnp.logical_not(here))(lambda: body(theirs))


def conv(green_pair, polarization, received, sums, place, piece, per_side, energies, factor, later=0, target=None):
    _, slots, _, rows, _ = polarization.shape
    block = row_block(rows)
    first = piece[0]
    wide = pl.BlockSpec((2, slots, 1, block, LANES), lambda j, r, s: (0, 0, 0, r, first + j * per_side))
    shape = (energies, block, 2 * LANES)
    specs = [
        pl.BlockSpec(shape, lambda j, r, s: (0, jnp.where(s[3] == j, r, 0), 0)),
        pl.BlockSpec(shape, lambda j, r, s: (0, jnp.where(s[3] == j, 0, r), 0)),
        wide,
    ]
    specs += [pl.BlockSpec((1, 2, slots, block, LANES), lambda j, r, s: (j, 0, 0, r, 0))] * len(received)
    groups_in = later + 1 if later else 1
    specs += [pl.BlockSpec((1, groups_in, 2, slots, block, LANES), lambda j, r, s: (j, 0, 0, 0, r, 0))] * len(sums)
    operands = [place, *green_pair, polarization, *received, *sums]
    aliases = {}
    if later:
        out_spec = pl.BlockSpec((1, later, 2, slots, block, LANES), lambda j, r, s: (j, 0, 0, 0, r, 0))
        out_shape = (len(piece), later, 2, slots, rows, LANES)
    else:
        out_spec, out_shape = wide, polarization.shape
        if target is not None:
            aliases = {len(operands): 0}
            operands.append(target)
            specs.append(pl.BlockSpec(memory_space=pl.ANY))
    plan = (slots, energies, factor, len(received), len(sums), later, first)
    return pl.pallas_call(
        functools.partial(conv_kernel, plan),
        grid_spec=pltpu.PrefetchScalarGridSpec(
            num_scalar_prefetch=1, grid=(len(piece), rows // block), in_specs=specs, out_specs=out_spec
        ),
        out_shape=jax.ShapeDtypeStruct(out_shape, polarization.dtype),
        input_output_aliases=aliases,
        compiler_params=pltpu.CompilerParams(vmem_limit_bytes=VMEM_BYTES),
        cost_estimate=pl.CostEstimate(flops=1024, bytes_accessed=1024, transcendentals=0),
        name="ahead" if later else "here",
    )(*operands)


def shards(coupling, block_mask, levels, dwell, polarization):
    groups, slices = lax.axis_size("energy"), lax.axis_size("cuts")
    _, slots, _, rows, columns = polarization.shape
    energies = groups * slots
    half = groups // 2
    factor = math.sqrt(columns / energies)
    chunks = pl.cdiv(columns, LANES)
    sharing = math.gcd(slices, 2)
    per_side = pl.cdiv(chunks, sharing)
    pieces = [[c for c in (side * per_side + k for side in range(sharing)) if c < chunks] for k in range(per_side)]
    as_sums = [0] if half > 0 else []

    def cut(k, after=None):
        values = polarization if after is None else lax.optimization_barrier((polarization, after))[0]
        parts = []
        for chunk in pieces[k]:
            part = values[:, :, 0, :, chunk * LANES : (chunk + 1) * LANES]
            parts.append(jnp.pad(part, ((0, 0), (0, 0), (0, 0), (0, LANES - part.shape[-1]))))
        return jnp.stack(parts)

    def send(values, pairs):
        return lax.ppermute(values, "energy", pairs)

    blocks = block_mask.shape[1]
    member = jnp.arange(rows)[:, None] // (rows // blocks) == jnp.arange(blocks)[None, :]
    member = member.astype(jnp.bfloat16)
    spread = jnp.dot(jnp.dot(member, block_mask[0].astype(jnp.bfloat16)), member.T)
    swap = [(i, i ^ 1) for i in range(slices)]
    couplings = lax.all_gather(coupling[0] * spread, "cuts")
    spectra = lax.all_gather(jnp.concatenate([levels, dwell]), "cuts")
    energy = jnp.arange(energies, dtype=jnp.int32).astype(jnp.float32)
    phases = (energy[None, :, None] - spectra[:, 0, None, :]) * spectra[:, 1, None, :]
    turns = jnp.stack([jnp.cos(phases), jnp.sin(phases)], axis=2).reshape(slices, 2 * energies, rows)
    turns = jnp.swapaxes(lax.optimization_barrier(turns), 1, 2)

    index = lax.axis_index("cuts")
    side_here = lax.rem(index, sharing)
    partner = index + (1 - 2 * side_here if sharing == 2 else 0)
    greens = {}
    queue = [1, 0, 2] if per_side == 3 else list(range(per_side))
    for k in queue:
        column = jnp.minimum(side_here * per_side + k, chunks - 1)
        place = jnp.stack([column, index, partner, side_here]).astype(jnp.int32)
        mine, other = chain(couplings, turns, place, energies)
        if sharing == 2:
            other = lax.ppermute(other, "cuts", swap)
        greens[k] = (mine, other)

    group = lax.axis_index("energy")
    received = [[] for _ in pieces]
    if half == 2 and groups == 4 and per_side == 3:
        forward = [(0, 1), (1, 2)]
        at_one, at_two = group == 1, group == 2
        a = send(jnp.where(at_one, cut(1), cut(0)), forward + [(2, 3)])
        b = send(cut(1, spectra), [(0, 2)])
        c = send(jnp.where(at_one, cut(2, spectra), cut(1, spectra)), forward)
        d = send(cut(2, (a, b, greens[queue[0]][0])), [(0, 2)])
        e = send(cut(2, d), [(0, 1)])
        received[0] = [jnp.where(at_two, jnp.zeros_like(a), a)]
        received[1] = [jnp.where(at_two, a, c), b]
        received[2] = [jnp.where(at_two, c, e), d]
    else:
        for k in range(per_side):
            for hop in range(1, max(half, groups - half) if k in as_sums else half + 1):
                if k in as_sums:
                    pairs = [(z, z + hop) for z in range(groups - hop) if (z < half) == (z + hop < half)]
                else:
                    pairs = [(z, z + hop) for z in range(half + 1 - hop)]
                received[k].append(send(cut(k), pairs))

    sums = [[] for _ in pieces]
    for k in queue:
        piece = pieces[k]
        run = functools.partial(
            conv, greens[k], polarization, place=place, piece=piece, per_side=per_side, energies=energies, factor=factor
        )
        if k in as_sums:
            partial = run(received[k][: half - 1], [], later=groups - half)
            for hop in reversed(range(groups - half)):
                sums[k].append(send(partial[:, hop : hop + 1], [(half - 1, half + hop)]))
        else:
            got = []
            for hop in range(1, groups - half):
                partial = run(received[k] if hop == 1 else [], got, later=groups - half - hop)
                got = [send(partial, [(half + hop - 1, half + hop)])]
                sums[k].append(got[0][:, :1])

    sigma = None
    for k in [k for k in queue if k not in as_sums] + as_sums:
        sigma = conv(
            greens[k], polarization, received[k], sums[k], place, pieces[k], per_side, energies, factor, 0, sigma
        )
    return sigma


def solution(mesh):
    return jax.shard_map(
        shards,
        mesh=mesh,
        in_specs=(
            P("cuts", None, None),
            P("cuts", None, None),
            P("cuts", None),
            P("cuts", None),
            P(None, "energy", "cuts", None, None),
        ),
        out_specs=P(None, "energy", "cuts", None, None),
        check_vma=False,
    )
```

```python
import functools
import math

import jax
import jax.numpy as jnp
from jax import lax
from jax.experimental import pallas as pl
from jax.experimental.pallas import tpu as pltpu
from jax.sharding import PartitionSpec as P

LANES = 128
WIDE = 2 * LANES
VMEM_BYTES = 26 * 1024 * 1024
COST = pl.CostEstimate(flops=1024, bytes_accessed=1024, transcendentals=0)


def row_step(rows):
    return 16 if rows % 16 == 0 else rows


def row_block(rows):
    for parts in (3, 5, 2):
        if rows % (16 * parts) == 0:
            return rows // parts
    return rows


def scalars(*values):
    return jnp.stack([jnp.asarray(v, jnp.int32) for v in values])


def tie(value, *after):
    return lax.optimization_barrier((value, after))[0] if after else value


def chain_kernel(counts, at, place, first, couple, turns, state):
    step = pl.program_id(0)

    def turned(real, imag, e):
        cosine = turns[0, :, 2 * e : 2 * e + 1]
        sine = turns[0, :, 2 * e + 1 : 2 * e + 2]
        if imag is None:
            return cosine * real, -sine * real
        return cosine * real + sine * imag, cosine * imag - sine * real

    def keep(e, pair):
        state[e, :, :WIDE] = pair[0].astype(jnp.bfloat16)
        state[e, :, WIDE:] = pair[1].astype(jnp.bfloat16)

    def begin(count):
        start = first[0].astype(jnp.float32)
        for e in range(count):
            keep(e, turned(start, None, e))
        for e in range(count, state.shape[0]):
            state[e] = jnp.zeros(state.shape[1:], state.dtype)

    def advance(count):
        for e in range(count):
            product = jnp.dot(couple[0], state[e], preferred_element_type=jnp.float32)
            keep(e, turned(product[:, :WIDE], product[:, WIDE:], e))

    for count in counts:
        asked = place[at[2]] == count
        pl.when(jnp.logical_and(asked, step == 0))(functools.partial(begin, count))
        going = jnp.logical_and(step > 0, step <= place[at[1]])
        pl.when(jnp.logical_and(asked, going))(functools.partial(advance, count))


def chain(couplings, turns, energies, place, at, counts):
    count, rows, _ = couplings.shape
    shape = (energies, rows, 2 * WIDE)
    return pl.pallas_call(
        functools.partial(chain_kernel, counts, at),
        grid_spec=pltpu.PrefetchScalarGridSpec(
            num_scalar_prefetch=1,
            grid=(count,),
            in_specs=[
                pl.BlockSpec((1, rows, WIDE), lambda i, s: (0, 0, s[at[0]])),
                pl.BlockSpec((1, rows, rows), lambda i, s: (jnp.minimum(i, s[at[1]]), 0, 0)),
                pl.BlockSpec((1, rows, 2 * energies), lambda i, s: (i, 0, 0)),
            ],
            out_specs=pl.BlockSpec(shape, lambda i, s: (0, 0, 0)),
        ),
        out_shape=jax.ShapeDtypeStruct(shape, jnp.bfloat16),
        compiler_params=pltpu.CompilerParams(vmem_limit_bytes=VMEM_BYTES),
        cost_estimate=COST,
        name="chain",
    )(place, couplings, couplings, turns)


def convolved(green, sources, slots, energies):
    out = []
    for e in range(slots):
        real, imag = None, None
        for shift, values in sources:
            for w in range(slots):
                g = shift * slots + e - w
                if g < 0 or g >= energies:
                    continue
                gr, gi = green(g)
                pr, pi = values(w)
                a, b = gr * pr - gi * pi, gr * pi + gi * pr
                real, imag = (a, b) if real is None else (real + a, imag + b)
        out.append((real, imag))
    return out


def by_tiles(rows, body):
    step = row_step(rows)

    def one(r, carry):
        for lane in range(0, WIDE, LANES):
            body(pl.ds(pl.multiple_of(r * step, step), step), lane)
        return carry

    lax.fori_loop(0, rows // step, one, 0)


def remembered(read):
    seen = {}

    def get(i):
        if i not in seen:
            seen[i] = tuple(part.astype(jnp.float32) for part in read(i))
        return seen[i]

    return get


def conv_kernel(plan, place, green_ref, own, *refs):
    slots, energies, factor, shifts, weighed, later = plan
    received, sums = refs[: len(shifts)], list(refs[len(shifts) : len(shifts) + sum(map(len, weighed))])
    outs = refs[-len(weighed) :]
    sums = [[(sums.pop(0), *how) for how in group] for group in weighed]

    def tile(rows, lane):
        here = slice(lane, lane + LANES)
        there = slice(WIDE + lane, WIDE + lane + LANES)

        def values(i):
            def read(w):
                pair = [received[i][0, part, w, rows, here].astype(jnp.float32) for part in range(2)]
                weight = shifts[i][1]
                return pair if weight is None else [part * place[weight].astype(jnp.float32) for part in pair]

            return read

        green = remembered(lambda g: (green_ref[g, rows, here], green_ref[g, rows, there]))
        terms = [(0, remembered(lambda w: (own[0, w, 0, rows, here], own[1, w, 0, rows, here])))]
        terms += [(shift, remembered(values(i))) for i, (shift, _) in enumerate(shifts)]
        for hop, out in enumerate(outs):
            ahead = [(shift + (hop + 1 if later else 0), read) for shift, read in terms]
            for e, pair in enumerate(convolved(green, ahead, slots, energies)):
                for part, total in enumerate(pair):
                    total = total * factor
                    for ref, weight, instead in sums[hop]:
                        got = ref[0, part, e, rows, here].astype(jnp.float32)
                        if instead:
                            total = jnp.where(place[weight] == 1, got, total)
                        else:
                            total = total + (got if weight is None else got * place[weight].astype(jnp.float32))
                    if later:
                        out[0, part, e, rows, here] = total.astype(out.dtype)
                    else:
                        out[part, e, 0, rows, here] = total.astype(out.dtype)

    by_tiles(own.shape[3], tile)


def conv(green, polarization, place, piece, received, sums, factor, later=0, target=None):
    _, slots, _, rows, _ = polarization.shape
    energies = green.shape[0]
    block = row_block(rows)
    most = max([0] + [v[1] for v in received]) + later
    used = min(energies, (most + 1) * slots)
    wide = pl.BlockSpec((2, slots, 1, block, WIDE), lambda r, s: (0, 0, 0, r, s[piece]))
    part = pl.BlockSpec((1, 2, slots, block, WIDE), lambda r, s: (0, 0, 0, r, 0))
    specs = [pl.BlockSpec((used, block, 2 * WIDE), lambda r, s: (0, r, 0)), wide]
    for values, _, which, _ in received:
        specs.append(
            pl.BlockSpec((1, 2, slots, block, WIDE), lambda r, s, which=which: (s[which], 0, 0, r, 0))
        )
    flat = [v for group in sums for v in group]
    specs += [part] * len(flat)
    operands = [place, green, polarization, *(v[0] for v in received), *(v[0] for v in flat)]
    aliases = {}
    if later:
        out_specs = [part] * later
        out_shape = [jax.ShapeDtypeStruct((1, 2, slots, rows, WIDE), polarization.dtype)] * later
    else:
        out_specs, out_shape = [wide], [jax.ShapeDtypeStruct(polarization.shape, polarization.dtype)]
        if target is not None:
            aliases = {len(operands): 0}
            operands.append(target)
            specs.append(pl.BlockSpec(memory_space=pl.ANY))
    shifts = tuple((v[1], v[3]) for v in received)
    weighed = tuple(tuple(v[1:] for v in group) for group in sums)
    result = pl.pallas_call(
        functools.partial(conv_kernel, (slots, used, factor, shifts, weighed, later)),
        grid_spec=pltpu.PrefetchScalarGridSpec(
            num_scalar_prefetch=1, grid=(rows // block,), in_specs=specs, out_specs=out_specs
        ),
        out_shape=out_shape,
        input_output_aliases=aliases,
        compiler_params=pltpu.CompilerParams(vmem_limit_bytes=VMEM_BYTES),
        cost_estimate=COST,
        name="ahead" if later else "here",
    )(*operands)
    return result if later else result[0]


def take_kernel(place, values, out):
    out[0] = values[:, :, 0]


def take(polarization, place, piece, count=1):
    _, slots, _, rows, _ = polarization.shape
    return pl.pallas_call(
        take_kernel,
        grid_spec=pltpu.PrefetchScalarGridSpec(
            num_scalar_prefetch=1,
            grid=(count,),
            in_specs=[pl.BlockSpec((2, slots, 1, rows, WIDE), lambda j, s: (0, 0, 0, 0, s[piece] + j))],
            out_specs=pl.BlockSpec((1, 2, slots, rows, WIDE), lambda j, s: (j, 0, 0, 0, 0)),
        ),
        out_shape=jax.ShapeDtypeStruct((count, 2, slots, rows, WIDE), polarization.dtype),
        compiler_params=pltpu.CompilerParams(vmem_limit_bytes=VMEM_BYTES),
        cost_estimate=COST,
        name="take",
    )(place, polarization)


def finish_kernel(place, base, got, out):
    total = base[...].astype(jnp.float32) + got[0][:, :, None].astype(jnp.float32)
    out[...] = total.astype(out.dtype)


def finish(sigma, got, place, piece):
    _, slots, _, rows, _ = sigma.shape
    block = row_block(rows)
    wide = pl.BlockSpec((2, slots, 1, block, WIDE), lambda r, s: (0, 0, 0, r, s[piece]))
    part = pl.BlockSpec((1, 2, slots, block, WIDE), lambda r, s: (0, 0, 0, r, 0))
    return pl.pallas_call(
        finish_kernel,
        grid_spec=pltpu.PrefetchScalarGridSpec(
            num_scalar_prefetch=1, grid=(rows // block,), in_specs=[wide, part], out_specs=wide
        ),
        out_shape=jax.ShapeDtypeStruct(sigma.shape, sigma.dtype),
        input_output_aliases={1: 0},
        compiler_params=pltpu.CompilerParams(vmem_limit_bytes=VMEM_BYTES),
        cost_estimate=COST,
        name="finish",
    )(place, sigma, got)


def shards(coupling, block_mask, levels, dwell, polarization):
    groups, slices = lax.axis_size("energy"), lax.axis_size("cuts")
    _, slots, _, rows, columns = polarization.shape
    energies = groups * slots
    half = groups // 2
    factor = math.sqrt(columns / energies)
    pieces = pl.cdiv(columns, WIDE)
    staged = groups == 4 and pieces == 3
    group = lax.axis_index("energy")
    zero, one, two, three = (group == z for z in range(4))

    early = jnp.where(one, 0, 1)
    middle = jnp.logical_or(one, two)
    odd = jnp.logical_or(one, three)
    lookup = {
        "slice": lax.axis_index("cuts"),
        "first": jnp.where(one, 1, 0),
        "early": early,
        "late": 1 - early,
        "last": jnp.where(two, 1 - early, 2),
        "all": energies,
        "count_a": jnp.where(middle, energies, slots),
        "count_b": jnp.where(two, energies, jnp.where(one, 2 * slots, slots)),
        "count_c": jnp.where(odd, 2 * slots, slots),
        "one": one,
        "two": two,
        "three": three,
        "middle": middle,
        "odd": odd,
    }
    at = {name: pieces + i for i, name in enumerate(lookup)}
    place = scalars(*range(pieces), *lookup.values())

    def send(values, pairs):
        return lax.ppermute(values, "energy", pairs)

    blocks = block_mask.shape[1]
    member = jnp.arange(rows)[:, None] // (rows // blocks) == jnp.arange(blocks)[None, :]
    member = member.astype(jnp.bfloat16)
    spread = jnp.dot(jnp.dot(member, block_mask[0].astype(jnp.bfloat16)), member.T)
    couplings = lax.all_gather(coupling[0] * spread, "cuts")
    spectrum = jnp.concatenate([levels, dwell])
    if staged:
        load_a = take(polarization, place, at["first"], 2)
        a = send(load_a, [(0, 1), (1, 2), (2, 3)])
        load_b = take(polarization, tie(place, load_a), 1)
        b = send(load_b, [(0, 2)])
        load_d = take(polarization, tie(place, load_b), 2)
        spectrum = tie(spectrum, load_d)
    spectra = lax.all_gather(spectrum, "cuts")
    energy = jnp.arange(energies, dtype=jnp.int32).astype(jnp.float32)
    phases = (energy[None, :, None] - spectra[:, 0, None, :]) * spectra[:, 1, None, :]
    turns = jnp.stack([jnp.cos(phases), jnp.sin(phases)], axis=2).reshape(slices, 2 * energies, rows)
    turns = jnp.swapaxes(lax.optimization_barrier(turns), 1, 2)

    def propagators(piece, count, counts, *after):
        return chain(couplings, turns, energies, tie(place, *after), (piece, at["slice"], count), counts)

    if staged:
        counts = (slots, 2 * slots, energies)
        green_a = propagators(at["early"], at["count_a"], counts)
        load_d = tie(load_d, green_a, a, b)
        d = send(load_d, [(0, 2)])
        ahead_a = conv(green_a, polarization, place, at["early"], [(a, 1, 0, None), (b, 2, 0, None)], [[], []], factor, 2)
        f = send(ahead_a[0], [(2, 3)])
        green_b = propagators(2, at["count_b"], counts, ahead_a)
        g = send(ahead_a[1], [(1, 3)])
        ahead_b = conv(
            green_b, polarization, place, 2, [(a, 1, 1, None), (d, 2, 0, None)], [[(ahead_a[0], at["one"], True)]], factor, 1
        )
        h = send(ahead_b[0], [(1, 2), (2, 3)])
        e = send(load_d, [(0, 1)])
        green_c = propagators(at["late"], at["count_c"], counts, ahead_b)
        sources = [(a, 1, 0, at["middle"]), (b, 2, 0, None)]
        sigma = conv(
            green_a, polarization, tie(place, green_c), at["early"], sources, [[(f, at["three"], False)]], factor
        )
        sources = [(a, 1, 1, at["two"]), (e, 1, 0, None), (d, 2, 0, None)]
        sigma = conv(green_b, polarization, place, 2, sources, [[]], factor, 0, sigma)
        sources = [(a, 1, at["first"], at["odd"])]
        sigma = conv(green_c, polarization, place, at["late"], sources, [[(g, None, False)]], factor, 0, sigma)
        return finish(sigma, h, place, at["last"])

    sigma = None
    for piece in range(pieces):
        green = propagators(piece, at["all"], (energies,))
        received, sums = [], []
        within = piece == 0 and half > 0
        for hop in range(1, max(half, groups - half) if within else half + 1):
            if within:
                pairs = [(z, z + hop) for z in range(groups - hop) if (z < half) == (z + hop < half)]
            else:
                pairs = [(z, z + hop) for z in range(half + 1 - hop)]
            received.append((send(take(polarization, place, piece), pairs), hop, 0, None))
        if within:
            later = groups - half
            partial = conv(green, polarization, place, piece, received[: half - 1], [[]] * later, factor, later)
            sums = [(send(values, [(half - 1, half + hop)]), None, False) for hop, values in enumerate(partial)]
        else:
            carried = [[]] * (groups - half)
            for hop in range(1, groups - half):
                later = groups - half - hop
                sources = received if hop == 1 else []
                partial = conv(green, polarization, place, piece, sources, carried[1:], factor, later)
                carried = [[(send(values, [(half + hop - 1, half + hop)]), None, False)] for values in partial]
                sums += carried[0]
        sigma = conv(green, polarization, place, piece, received, [sums], factor, 0, sigma)
    return sigma


def solution(mesh):
    return jax.shard_map(
        shards,
        mesh=mesh,
        in_specs=(
            P("cuts", None, None),
            P("cuts", None, None),
            P("cuts", None),
            P("cuts", None),
            P(None, "energy", "cuts", None, None),
        ),
        out_specs=P(None, "energy", "cuts", None, None),
        check_vma=False,
    )
```
